768 devices in a mesh: grp: 8 (over z_hi, x), row: 96 (over y, z_lo, core).
Axes of the slice: x: 4, y: 8, z: 12 (z_hi: 2, z_lo: 6; z = z_hi * 6 + z_lo), core: 2. Of those that a mesh axis runs over, the one named last changes fastest.
Arguments:
- features: bfloat16 [73728, 128], P('row'), may hold values from -6 to 6
- dest_plan: int32 [96, 48], replicated, may hold values from 0 to 95, as said below
- adj_tiles: bfloat16 [24, 768, 73728], P(None, 'grp', 'row'), may hold values from -0.046875 to 0.046875
- tile_cols: int32 [96, 24], P('row'), may hold values from 0 to 95, as said below
- tile_count: int32 [96], P('row'), may hold values from 12 to 24, as said below
- grad_out: bfloat16 [73728, 256], P('row'), may hold values from -0.0234375 to 0.0234375
- weight: bfloat16 [128, 256], replicated, may hold values from -0.5 to 0.5
Outputs:
- hidden_out: bfloat16 [73728, 256], P('row')
- weight_grad: float32 [128, 256], replicated
The draws below stay inside these ranges and needn't reach their ends.
Inputs may be any that keep to these rules, and one draw needn't show every extreme that they name: `dest_plan`: row s holds 48 different blocks, none equal to s; every block appears exactly 48 times in all. `tile_cols`: each row holds 24 different column blocks. `tile_count`: some row block uses all 24 slots in every draw.
All inputs are finite; a program needn't handle non-finite values.
Results may differ from the reference program's by a relative error of at most 0.0056.
Values may be sent and summed in bfloat16 or wider, within the bound.
No kernel may reach another device: no remote copies, remote signals or barrier semaphores. Data moves between devices by JAX's collectives and lax.ppermute only.
A program may use at most 32 MiB of HBM per device.

```python
import jax
import jax.numpy as jnp
from jax import lax

F_IN = 128
HID = 256
KEEP = 576
MIG = 48
SB = 4
BR = 768
KT = 24
NODES = 73728
N_ROW = 96


def draw_dest_plan(key, part):
    key = jax.random.fold_in(key, 11)
    relabel_key, shift_key = jax.random.split(key)
    labels = jax.random.permutation(relabel_key, jnp.arange(N_ROW, dtype=jnp.int32))
    places = jnp.zeros((N_ROW,), jnp.int32).at[labels].set(jnp.arange(N_ROW, dtype=jnp.int32))
    shifts = jax.random.permutation(shift_key, jnp.arange(1, N_ROW, dtype=jnp.int32))[:MIG]
    return labels[(places[:, None] + shifts[None, :]) % N_ROW].astype(jnp.int32)


def draw_tile_cols(key, part):
    key = jax.random.fold_in(key, 23)
    scores = jax.random.randint(key, (N_ROW, N_ROW), 0, 1 << 20)
    scores = scores * N_ROW + jnp.arange(N_ROW, dtype=jnp.int32)[None, :]
    return jnp.argsort(scores, axis=1, stable=True)[:, :KT].astype(jnp.int32)


def draw_tile_count(key, part):
    key = jax.random.fold_in(key, 37)
    count_key, full_key = jax.random.split(key)
    counts = jax.random.randint(count_key, (N_ROW,), (KT + 1) // 2, KT + 1)
    fullest = jax.random.randint(full_key, (), 0, N_ROW)
    return jnp.where(jnp.arange(N_ROW) == fullest, KT, counts).astype(jnp.int32)


def block_levels(rng, shape, pieces, smallest, high):
    def one(axis_at, shards_of):
        heights = jax.random.uniform(jax.random.fold_in(jax.random.fold_in(rng, 6), axis_at), (shards_of,), jnp.float32, smallest / len(pieces), high / len(pieces))
        return jnp.repeat(jnp.exp(heights), shape[axis_at] // shards_of).reshape((-1,) + (1,) * (len(shape) - axis_at - 1))

    factor_of = one(*pieces[0])
    for cut in pieces[1:]:
        factor_of = factor_of * one(*cut)
    return factor_of


def bell_draw(rng, extent, width, reach, pieces=(), held_as=jnp.bfloat16):
    drawn = jax.random.normal(rng, extent, jnp.float32) * width
    if len(pieces) > 0:
        drawn = block_levels(rng, extent, pieces, -0.22, 0.18) * drawn
    return jnp.clip(drawn, min=-reach, max=reach).astype(held_as)


def setup_inputs(seed: int = 0) -> dict:
    key_list = jax.random.split(jax.random.key(seed), 8)
    features = bell_draw(key_list[0], (NODES, F_IN), 1.0, 6.0, ((0, 96),))
    dest_plan = draw_dest_plan(jax.random.fold_in(key_list[7], 71), 0)
    adj_tiles = bell_draw(key_list[2], (KT, BR, NODES), (KT * BR) ** -0.5, 0.046875, ((1, 8), (2, 96)))
    tile_cols = draw_tile_cols(jax.random.fold_in(key_list[7], 71), 0)
    tile_count = draw_tile_count(jax.random.fold_in(key_list[7], 71), 0)
    grad_out = bell_draw(key_list[5], (NODES, HID), NODES ** -0.5, 0.0234375, ((0, 96),))
    weight = bell_draw(key_list[6], (F_IN, HID), F_IN ** -0.5, 0.5)
    return dict(features=features, dest_plan=dest_plan, adj_tiles=adj_tiles, tile_cols=tile_cols, tile_count=tile_count, grad_out=grad_out, weight=weight)


def reference(features, dest_plan, adj_tiles, tile_cols, tile_count, grad_out, weight):
    blocks = features.reshape(N_ROW, BR, F_IN)
    leaving = blocks[:, KEEP:, :].reshape(N_ROW, MIG, SB * F_IN).astype(jnp.float32)
    owners = jnp.arange(N_ROW, dtype=jnp.int32)
    positions = jnp.arange(MIG, dtype=jnp.int32)

    def arrive(target):
        hits = (dest_plan == target).astype(jnp.float32)
        sent = jnp.einsum("sj,sjc->sc", hits, leaving)
        flags = jnp.sum(hits, axis=1) > 0
        sender_rank = (jnp.cumsum(flags.astype(jnp.int32), dtype=jnp.int32) - 1).astype(jnp.int32)
        chooser = (flags[None, :] & (sender_rank[None, :] == positions[:, None])).astype(jnp.float32)
        return jnp.dot(chooser, sent).reshape(MIG * SB, F_IN)

    incoming = lax.map(arrive, owners).astype(jnp.bfloat16)
    relocated = jnp.concatenate([blocks[:, :KEEP, :], incoming], axis=1)

    def aggregate(block_index):
        start = (block_index * BR).astype(jnp.int32)
        tiles = lax.dynamic_slice_in_dim(adj_tiles, start, BR, 2).astype(jnp.float32)
        column_ids = tile_cols[block_index]
        live_slots = jnp.arange(KT, dtype=jnp.int32) < tile_count[block_index]
        picked = jnp.take(relocated, column_ids, axis=0).astype(jnp.float32)
        picked = jnp.where(live_slots[:, None, None], picked, jnp.zeros_like(picked))
        return jnp.einsum("kjn,kjf->nf", tiles, picked)

    summed = lax.map(aggregate, owners).reshape(NODES, F_IN)
    aggregated = summed.astype(jnp.bfloat16)
    projected = jnp.dot(aggregated, weight, preferred_element_type=jnp.float32)
    sig = jax.nn.sigmoid(projected)
    hidden_out = (projected * sig).astype(jnp.bfloat16)
    slope = sig * (1.0 + projected * (1.0 - sig))
    masked = (grad_out.astype(jnp.float32) * slope).astype(jnp.bfloat16)
    weight_grad = jnp.dot(aggregated.T, masked, preferred_element_type=jnp.float32)
    return hidden_out, weight_grad
```

```python
import jax
import jax.numpy as jnp
from jax import lax
from jax.sharding import Mesh, PartitionSpec as P

KEEP = 576
GRP = ("zh", "x")
ROW = ("y", "zl", "c")
CHIPS = ("y", "zl")
FINE = (2, 4, 8, 6, 2)


def exchange(pieces, axes):
    return lax.all_to_all(pieces, axes, split_axis=0, concat_axis=0, tiled=True)


def spread(value, axes):
    copies = jnp.broadcast_to(value[None], (lax.axis_size(axes),) + value.shape)
    return exchange(copies, axes)


def relocate(features, dest_plan, own_row):
    block_rows, feat_width = features.shape
    row_count, leaving = dest_plan.shape
    part_rows = (block_rows - KEEP) // leaving
    targets = lax.dynamic_index_in_dim(dest_plan, own_row, 0, keepdims=False)
    owners = jnp.arange(row_count, dtype=jnp.int32)
    outgoing = (targets[None, :] == owners[:, None]).astype(jnp.bfloat16)
    leaving_rows = features[KEEP:].reshape(leaving, part_rows * feat_width)
    packed = jnp.dot(outgoing, leaving_rows, preferred_element_type=jnp.float32).astype(jnp.bfloat16)
    arrived = exchange(packed, ROW)
    senders = jnp.any(dest_plan == own_row, axis=1)
    sender_rank = jnp.sum(
        (senders[None, :] & (owners[None, :] < owners[:, None])).astype(jnp.int32), axis=1
    )
    positions = jnp.arange(leaving, dtype=jnp.int32)
    chooser = (senders[None, :] & (sender_rank[None, :] == positions[:, None])).astype(jnp.bfloat16)
    incoming = jnp.dot(chooser, arrived, preferred_element_type=jnp.float32).astype(jnp.bfloat16)
    return jnp.concatenate(
        [features[:KEEP], incoming.reshape(leaving * part_rows, feat_width)], axis=0
    )


def on_device(features, dest_plan, adj_tiles, tile_cols, tile_count, grad_out, weight):
    block_rows, feat_width = features.shape
    hid = weight.shape[1]
    group_count = lax.axis_size(GRP)
    own_row = lax.axis_index(ROW)
    own_group = lax.axis_index(GRP)
    own_core = lax.axis_index("c")
    slice_rows = block_rows // group_count
    relocated = relocate(features, dest_plan, own_row)
    own_slice = lax.dynamic_slice_in_dim(relocated, own_group * slice_rows, slice_rows, 0)

    same_core = spread(own_slice, CHIPS).reshape(-1, slice_rows, feat_width)
    other_core = lax.ppermute(same_core, "c", [(0, 1), (1, 0)])
    gathered = jnp.concatenate([same_core, other_core], axis=0)
    column_ids = tile_cols[0]
    places = column_ids // 2 + jnp.where(column_ids % 2 == own_core, 0, same_core.shape[0])
    live_slots = jnp.arange(column_ids.shape[0], dtype=jnp.int32) < tile_count[0]
    picked = jnp.take(gathered, places, axis=0)
    picked = jnp.where(live_slots[:, None, None], picked, jnp.zeros_like(picked))

    partial_value = lax.dot_general(
        picked, adj_tiles, (((0, 1), (0, 1)), ((), ())), preferred_element_type=jnp.float32
    ).astype(jnp.bfloat16)
    terms = exchange(partial_value, GRP).reshape(group_count, -1, block_rows)
    own_feats = jnp.sum(terms.astype(jnp.float32), axis=0).astype(jnp.bfloat16)
    aggregated = spread(own_feats, GRP).reshape(feat_width, block_rows)

    projected = lax.dot_general(
        aggregated, weight, (((0,), (0,)), ((), ())), preferred_element_type=jnp.float32
    )
    sigmoid_part = jax.nn.sigmoid(projected)
    activated = (projected * sigmoid_part).astype(jnp.bfloat16)
    slope = sigmoid_part * (1.0 + projected * (1.0 - sigmoid_part))
    masked = (grad_out.astype(jnp.float32) * slope).astype(jnp.bfloat16)
    local_grad = jnp.dot(own_feats, masked, preferred_element_type=jnp.float32)

    y_terms = exchange(local_grad, "y").reshape(lax.axis_size("y"), -1, hid)
    chip_terms = spread(jnp.sum(y_terms, axis=0), ("zl", "c"))
    own_grad = jnp.sum(chip_terms.reshape((-1,) + y_terms.shape[1:]), axis=0)
    weight_grad = spread(own_grad, GRP + ("y",)).reshape(feat_width, hid)
    return (activated, weight_grad)


def solution(mesh):
    fine_mesh = Mesh(mesh.devices.reshape(FINE), GRP + ROW)
    in_specs = (
        P(ROW, None),
        P(),
        P(None, GRP, ROW),
        P(ROW, None),
        P(ROW),
        P(ROW, None),
        P(),
    )
    out_specs = (P(ROW, None), P())
    return jax.shard_map(
        on_device, mesh=fine_mesh, in_specs=in_specs, out_specs=out_specs, check_vma=False
    )
```

```python
import jax
import jax.numpy as jnp
from jax import lax
from jax.sharding import Mesh, PartitionSpec as P

KEEP = 576
GRP = ("zh", "x")
ROW = ("y", "zl", "c")
CHIPS = ("y", "zl")
FINE = (2, 4, 8, 6, 2)


def exchange(pieces, axes):
    return lax.all_to_all(pieces, axes, split_axis=0, concat_axis=0, tiled=True)


def spread(value, axes):
    copies = jnp.broadcast_to(value[None], (lax.axis_size(axes),) + value.shape)
    return exchange(copies, axes)


def relocate(features, dest_plan, own_row):
    block_rows, feat_width = features.shape
    row_count, leaving = dest_plan.shape
    part_rows = (block_rows - KEEP) // leaving
    targets = lax.dynamic_index_in_dim(dest_plan, own_row, 0, keepdims=False)
    owners = jnp.arange(row_count, dtype=jnp.int32)
    outgoing = (targets[None, :] == owners[:, None]).astype(jnp.bfloat16)
    leaving_rows = features[KEEP:].reshape(leaving, part_rows * feat_width)
    packed = jnp.dot(outgoing, leaving_rows, preferred_element_type=jnp.float32).astype(jnp.bfloat16)
    arrived = exchange(packed, ROW)
    senders = jnp.any(dest_plan == own_row, axis=1)
    sender_rank = jnp.sum(
        (senders[None, :] & (owners[None, :] < owners[:, None])).astype(jnp.int32), axis=1
    )
    positions = jnp.arange(leaving, dtype=jnp.int32)
    chooser = (senders[None, :] & (sender_rank[None, :] == positions[:, None])).astype(jnp.bfloat16)
    incoming = jnp.dot(chooser, arrived, preferred_element_type=jnp.float32).astype(jnp.bfloat16)
    return jnp.concatenate(
        [features[:KEEP], incoming.reshape(leaving * part_rows, feat_width)], axis=0
    )


def on_device(features, dest_plan, adj_tiles, tile_cols, tile_count, grad_out, weight):
    block_rows, feat_width = features.shape
    hid = weight.shape[1]
    group_count = lax.axis_size(GRP)
    own_row = lax.axis_index(ROW)
    own_group = lax.axis_index(GRP)
    own_core = lax.axis_index("c")
    slice_rows = block_rows // group_count
    relocated = relocate(features, dest_plan, own_row)
    own_slice = lax.dynamic_slice_in_dim(relocated, own_group * slice_rows, slice_rows, 0)

    same_core = spread(own_slice, CHIPS).reshape(-1, slice_rows, feat_width)
    other_core = lax.ppermute(same_core, "c", [(0, 1), (1, 0)])
    gathered = jnp.concatenate([same_core, other_core], axis=0)
    column_ids = tile_cols[0]
    places = column_ids // 2 + jnp.where(column_ids % 2 == own_core, 0, same_core.shape[0])
    live_slots = jnp.arange(column_ids.shape[0], dtype=jnp.int32) < tile_count[0]
    picked = jnp.take(gathered, places, axis=0)
    picked = jnp.where(live_slots[:, None, None], picked, jnp.zeros_like(picked))

    partial_value = lax.dot_general(
        picked, adj_tiles, (((0, 1), (0, 1)), ((), ())), preferred_element_type=jnp.float32
    ).astype(jnp.bfloat16)
    terms = exchange(partial_value, "x").reshape(lax.axis_size("x"), -1, block_rows)
    near = jnp.sum(terms.astype(jnp.float32), axis=0).astype(jnp.bfloat16)
    far = lax.ppermute(near, "zh", [(0, 1), (1, 0)])
    own_feats = (near.astype(jnp.float32) + far.astype(jnp.float32)).astype(jnp.bfloat16)
    aggregated = spread(own_feats, "x").reshape(feat_width, block_rows)

    projected = lax.dot_general(
        aggregated, weight, (((0,), (0,)), ((), ())), preferred_element_type=jnp.float32
    )
    sigmoid_part = jax.nn.sigmoid(projected)
    activated = (projected * sigmoid_part).astype(jnp.bfloat16)
    slope = sigmoid_part * (1.0 + projected * (1.0 - sigmoid_part))
    masked = (grad_out.astype(jnp.float32) * slope).astype(jnp.bfloat16)
    local_grad = jnp.dot(aggregated, masked, preferred_element_type=jnp.float32)

    ring_terms = exchange(local_grad, ("y", "c")).reshape(lax.axis_size(("y", "c")), -1, hid)
    line_terms = spread(jnp.sum(ring_terms, axis=0), "zl")
    own_grad = jnp.sum(line_terms.reshape((-1,) + ring_terms.shape[1:]), axis=0)
    weight_grad = spread(own_grad, ("y", "c")).reshape(feat_width, hid)
    return (activated, weight_grad)


def solution(mesh):
    fine_mesh = Mesh(mesh.devices.reshape(FINE), GRP + ROW)
    in_specs = (
        P(ROW, None),
        P(),
        P(None, GRP, ROW),
        P(ROW, None),
        P(ROW),
        P(ROW, None),
        P(),
    )
    out_specs = (P(ROW, None), P())
    return jax.shard_map(
        on_device, mesh=fine_mesh, in_specs=in_specs, out_specs=out_specs, check_vma=False
    )
```

```python
import functools

import jax
import jax.numpy as jnp
from jax import lax
from jax.experimental import pallas as pl
from jax.experimental.pallas import tpu as pltpu
from jax.sharding import Mesh, PartitionSpec as P

KEEP = 576
GRP = ("zh", "x")
ROW = ("y", "zl", "c")
FINE = (2, 4, 8, 6, 2)


def exchange(pieces, axes):
    return lax.all_to_all(pieces, axes, split_axis=0, concat_axis=0, tiled=True)


def spread(value, axes):
    copies = jnp.broadcast_to(value[None], (lax.axis_size(axes),) + value.shape)
    return exchange(copies, axes)


def vmem():
    return pl.BlockSpec(memory_space=pltpu.VMEM)


def smem():
    return pl.BlockSpec(memory_space=pltpu.SMEM)


def contract_last(first, second):
    return lax.dot_general(
        first, second, (((1,), (1,)), ((), ())), preferred_element_type=jnp.float32
    )


def grid_of(shape, axis):
    return lax.broadcasted_iota(jnp.int32, shape, axis)


def places_kernel(first_moving, held, role_ref, slot_ref, plan_ref, column_ref, mine_ref, theirs_ref, sent_ref):
    row_count, leaving = plan_ref.shape
    slot_count = column_ref.shape[1]
    half_rows = row_count // 2
    group, core, live = role_ref[0], role_ref[1], role_ref[2]
    half = jnp.maximum(group - first_moving, 0)

    eye = (grid_of((leaving, leaving), 0) == grid_of((leaving, leaving), 1)).astype(jnp.float32)
    plan = contract_last(eye.astype(jnp.bfloat16), plan_ref[...].astype(jnp.float32).astype(jnp.bfloat16))
    plan = plan.astype(jnp.int32)
    numbers = grid_of(plan.shape, 0) + 1
    for slot in range(slot_count):
        hits = jnp.where(plan == slot_ref[0, slot], numbers, 0)
        sent_ref[slot : slot + 1, :] = jnp.sum(hits.astype(jnp.float32), axis=0, keepdims=True)
    sent = sent_ref[...]

    square = (row_count, row_count)
    before = (grid_of(square, 1) < grid_of(square, 0)).astype(jnp.float32).astype(jnp.bfloat16)
    same = (grid_of(square, 1) == grid_of(square, 0)).astype(jnp.float32).astype(jnp.bfloat16)
    flags = jnp.where(sent > 0, 1.0, 0.0).astype(jnp.bfloat16)
    ranks = contract_last(before, flags).astype(jnp.int32)
    numbers = contract_last(same, sent.astype(jnp.bfloat16)).astype(jnp.int32) - 1

    source = grid_of(numbers.shape, 0)
    offset = (source >> 1) * held + jnp.where((source & 1) == core, 0, half_rows * held)
    local = numbers - half * held
    here = (numbers >= 0) & (local >= 0) & (local < held)
    none_held = row_count * held
    words = jnp.where(here, offset + local - none_held, 0)
    ranks = jnp.where(numbers >= 0, ranks, -1)

    columns = column_ref[...]
    column_base = (columns >> 1) * held + jnp.where((columns & 1) == core, 0, half_rows * held)
    dead = grid_of(columns.shape, 1) >= live
    for order in range(held):
        chosen = jnp.where(ranks == half * held + order, words, 0)
        moved = none_held + jnp.sum(chosen, axis=0, keepdims=True)
        stayed = column_base + order
        own = jnp.where(group >= first_moving, moved, stayed)
        mine_ref[order : order + 1, :] = jnp.where(dead, none_held, own)
        chosen = jnp.where(ranks == (1 - half) * held + order, words, 0)
        other = none_held + jnp.sum(chosen, axis=0, keepdims=True)
        theirs_ref[order : order + 1, :] = jnp.where(dead, none_held, other)


def part_places(role, columns, dest_plan, first_moving, held):
    shape = jax.ShapeDtypeStruct((held, columns.shape[1]), jnp.int32)
    return pl.pallas_call(
        functools.partial(places_kernel, first_moving, held),
        out_shape=(shape, shape),
        in_specs=[smem(), smem(), vmem(), vmem()],
        out_specs=(vmem(), vmem()),
        scratch_shapes=[pltpu.VMEM((columns.shape[1], dest_plan.shape[0]), jnp.float32)],
        cost_estimate=pl.CostEstimate(flops=4000000, bytes_accessed=50000, transcendentals=0),
    )(role, columns, dest_plan, columns)


def pick_kernel(place_ref, first_ref, second_ref, out_ref, held_ref, sems):
    half = first_ref.shape[0]
    first = pltpu.make_async_copy(first_ref, held_ref.at[pl.ds(0, half)], sems.at[0])
    second = pltpu.make_async_copy(second_ref, held_ref.at[pl.ds(half, half)], sems.at[1])
    first.start()
    second.start()
    held_ref[2 * half] = jnp.zeros(held_ref.shape[1:], held_ref.dtype)
    first.wait()
    second.wait()
    orders, slots = place_ref.shape

    def one_slot(slot, carry):
        for order in range(orders):
            out_ref[slot * orders + order] = held_ref[place_ref[order, slot]]
        return carry

    lax.fori_loop(0, slots, one_slot, 0)


def pick_parts(places, first, second):
    part = first.shape[1:]
    count = places.shape[0] * places.shape[1]
    return pl.pallas_call(
        pick_kernel,
        out_shape=jax.ShapeDtypeStruct((count,) + part, first.dtype),
        in_specs=[smem()] + [pl.BlockSpec(memory_space=pl.ANY)] * 2,
        out_specs=vmem(),
        scratch_shapes=[
            pltpu.VMEM((2 * first.shape[0] + 8,) + part, first.dtype),
            pltpu.SemaphoreType.DMA((2,)),
        ],
        compiler_params=pltpu.CompilerParams(vmem_limit_bytes=32 * 1024 * 1024),
        cost_estimate=pl.CostEstimate(flops=1000000, bytes_accessed=3000000, transcendentals=0),
    )(places, first, second)


def on_device(features, dest_plan, adj_tiles, tile_cols, tile_count, grad_out, weight):
    block_rows, feat_width = features.shape
    hid = weight.shape[1]
    own_group = lax.axis_index(GRP)
    leaving = dest_plan.shape[1]
    part_rows = (block_rows - KEEP) // leaving
    slice_rows = block_rows // lax.axis_size(GRP)
    held = slice_rows // part_rows
    first_moving = KEEP // slice_rows
    part_shape = (-1, part_rows, feat_width)

    own_slice = lax.dynamic_slice_in_dim(features, own_group * slice_rows, slice_rows, 0)
    same_core = spread(spread(own_slice, "zl"), "y").reshape(part_shape)
    other_core = lax.ppermute(same_core, "c", [(0, 1), (1, 0)])
    role = jnp.stack([own_group, lax.axis_index("c"), tile_count[0]])
    mine, theirs = part_places(role, tile_cols, dest_plan, first_moving, held)
    for_peer = pick_parts(theirs, same_core, other_core)
    from_peer = lax.ppermute(
        for_peer, GRP, [(first_moving, first_moving + 1), (first_moving + 1, first_moving)]
    )
    picked = pick_parts(mine, same_core, other_core) + from_peer
    picked = picked.reshape(adj_tiles.shape[0], slice_rows, feat_width)

    partial_value = lax.dot_general(
        picked, adj_tiles, (((0, 1), (0, 1)), ((), ())), preferred_element_type=jnp.float32
    ).astype(jnp.bfloat16)
    terms = exchange(partial_value, "x").reshape(lax.axis_size("x"), -1, block_rows)
    near = jnp.sum(terms.astype(jnp.float32), axis=0).astype(jnp.bfloat16)
    far = lax.ppermute(near, "zh", [(0, 1), (1, 0)])
    own_feats = (near.astype(jnp.float32) + far.astype(jnp.float32)).astype(jnp.bfloat16)
    aggregated = spread(own_feats, "x").reshape(feat_width, block_rows)

    projected = lax.dot_general(
        aggregated, weight, (((0,), (0,)), ((), ())), preferred_element_type=jnp.float32
    )
    sigmoid_part = jax.nn.sigmoid(projected)
    activated = (projected * sigmoid_part).astype(jnp.bfloat16)
    slope = sigmoid_part * (1.0 + projected * (1.0 - sigmoid_part))
    masked = (grad_out.astype(jnp.float32) * slope).astype(jnp.bfloat16)
    local_grad = jnp.dot(aggregated, masked, preferred_element_type=jnp.float32)

    ring_terms = exchange(local_grad, ("y", "c")).reshape(lax.axis_size(("y", "c")), -1, hid)
    line_terms = spread(jnp.sum(ring_terms, axis=0), "zl")
    own_grad = jnp.sum(line_terms.reshape((-1,) + ring_terms.shape[1:]), axis=0)
    weight_grad = spread(own_grad, ("y", "c")).reshape(feat_width, hid)
    return (activated, weight_grad)


def solution(mesh):
    fine_mesh = Mesh(mesh.devices.reshape(FINE), GRP + ROW)
    in_specs = (
        P(ROW, None),
        P(),
        P(None, GRP, ROW),
        P(ROW, None),
        P(ROW),
        P(ROW, None),
        P(),
    )
    out_specs = (P(ROW, None), P())
    return jax.shard_map(
        on_device, mesh=fine_mesh, in_specs=in_specs, out_specs=out_specs, check_vma=False
    )
```

```python
import functools

import jax
import jax.numpy as jnp
from jax import lax
from jax.experimental import pallas as pl
from jax.experimental.pallas import tpu as pltpu
from jax.sharding import Mesh, PartitionSpec as P

KEEP = 576
GRP = ("zh", "x")
ROW = ("y", "zl", "c")
FINE = (2, 4, 8, 6, 2)


def exchange(pieces, axes):
    return lax.all_to_all(pieces, axes, split_axis=0, concat_axis=0, tiled=True)


def spread(value, axes):
    copies = jnp.broadcast_to(value[None], (lax.axis_size(axes),) + value.shape)
    return exchange(copies, axes)


def vmem():
    return pl.BlockSpec(memory_space=pltpu.VMEM)


def smem():
    return pl.BlockSpec(memory_space=pltpu.SMEM)


def contract_last(first, second):
    return lax.dot_general(
        first, second, (((1,), (1,)), ((), ())), preferred_element_type=jnp.float32
    )


def grid_of(shape, axis):
    return lax.broadcasted_iota(jnp.int32, shape, axis)


def places_kernel(
    first_moving, held, group_ref, core_ref, live_ref, slot_ref, plan_ref, column_ref, mine_ref, theirs_ref, sent_ref
):
    leaving, row_count = plan_ref.shape
    slot_count = column_ref.shape[1]
    half_rows = row_count // 2
    group, core, live = group_ref[0], core_ref[0], live_ref[0]
    half = jnp.maximum(group - first_moving, 0)

    plan = plan_ref[...]
    numbers = grid_of(plan.shape, 0) + 1
    for slot in range(slot_count):
        hits = jnp.where(plan == slot_ref[0, slot], numbers, 0)
        sent_ref[slot : slot + 1, :] = jnp.sum(hits.astype(jnp.float32), axis=0, keepdims=True)
    sent = sent_ref[...]

    square = (row_count, row_count)
    before = (grid_of(square, 1) < grid_of(square, 0)).astype(jnp.float32).astype(jnp.bfloat16)
    same = (grid_of(square, 1) == grid_of(square, 0)).astype(jnp.float32).astype(jnp.bfloat16)
    flags = jnp.where(sent > 0, 1.0, 0.0).astype(jnp.bfloat16)
    ranks = contract_last(before, flags).astype(jnp.int32)
    numbers = contract_last(same, sent.astype(jnp.bfloat16)).astype(jnp.int32) - 1

    source = grid_of(numbers.shape, 0)
    offset = (source >> 1) * held + jnp.where((source & 1) == core, 0, half_rows * held)
    local = numbers - half * held
    here = (numbers >= 0) & (local >= 0) & (local < held)
    none_held = row_count * held
    words = jnp.where(here, offset + local - none_held, 0)
    ranks = jnp.where(numbers >= 0, ranks, -1)

    columns = column_ref[...]
    column_base = (columns >> 1) * held + jnp.where((columns & 1) == core, 0, half_rows * held)
    dead = grid_of(columns.shape, 1) >= live
    for order in range(held):
        chosen = jnp.where(ranks == half * held + order, words, 0)
        moved = none_held + jnp.sum(chosen, axis=0, keepdims=True)
        stayed = column_base + order
        own = jnp.where(group >= first_moving, moved, stayed)
        mine_ref[order : order + 1, :] = jnp.where(dead, none_held, own)
        chosen = jnp.where(ranks == (1 - half) * held + order, words, 0)
        other = none_held + jnp.sum(chosen, axis=0, keepdims=True)
        theirs_ref[order : order + 1, :] = jnp.where(dead, none_held, other)


def part_places(role, columns, dest_plan, first_moving, held):
    shape = jax.ShapeDtypeStruct((held, columns.shape[1]), jnp.int32)
    return pl.pallas_call(
        functools.partial(places_kernel, first_moving, held),
        out_shape=(shape, shape),
        in_specs=[smem(), smem(), smem(), smem(), vmem(), vmem()],
        out_specs=(vmem(), vmem()),
        scratch_shapes=[pltpu.VMEM((columns.shape[1], dest_plan.shape[0]), jnp.float32)],
        cost_estimate=pl.CostEstimate(flops=4000000, bytes_accessed=50000, transcendentals=0),
    )(*role, columns, dest_plan.T, columns)


def pick_kernel(place_ref, first_ref, second_ref, out_ref, held_ref, sems):
    half = first_ref.shape[0]
    first = pltpu.make_async_copy(first_ref, held_ref.at[pl.ds(0, half)], sems.at[0])
    second = pltpu.make_async_copy(second_ref, held_ref.at[pl.ds(half, half)], sems.at[1])
    first.start()
    second.start()
    held_ref[2 * half] = jnp.zeros(held_ref.shape[1:], held_ref.dtype)
    first.wait()
    second.wait()
    orders, slots = place_ref.shape

    def one_slot(slot, carry):
        for order in range(orders):
            out_ref[slot * orders + order] = held_ref[place_ref[order, slot]]
        return carry

    lax.fori_loop(0, slots, one_slot, 0)


def pick_parts(places, first, second):
    part = first.shape[1:]
    count = places.shape[0] * places.shape[1]
    return pl.pallas_call(
        pick_kernel,
        out_shape=jax.ShapeDtypeStruct((count,) + part, first.dtype),
        in_specs=[smem()] + [pl.BlockSpec(memory_space=pl.ANY)] * 2,
        out_specs=vmem(),
        scratch_shapes=[
            pltpu.VMEM((2 * first.shape[0] + 8,) + part, first.dtype),
            pltpu.SemaphoreType.DMA((2,)),
        ],
        compiler_params=pltpu.CompilerParams(vmem_limit_bytes=8 * 1024 * 1024),
        cost_estimate=pl.CostEstimate(flops=1000000, bytes_accessed=3000000, transcendentals=0),
    )(places, first, second)


def on_device(features, dest_plan, adj_tiles, tile_cols, tile_count, grad_out, weight):
    block_rows, feat_width = features.shape
    hid = weight.shape[1]
    own_group = lax.axis_index(GRP)
    leaving = dest_plan.shape[1]
    part_rows = (block_rows - KEEP) // leaving
    slice_rows = block_rows // lax.axis_size(GRP)
    held = slice_rows // part_rows
    first_moving = KEEP // slice_rows
    part_shape = (-1, part_rows, feat_width)

    own_slice = lax.dynamic_slice_in_dim(features, own_group * slice_rows, slice_rows, 0)
    same_core = spread(spread(own_slice, "zl"), "y").reshape(part_shape)
    role = (own_group.reshape(1), lax.axis_index("c").reshape(1), tile_count)
    mine, theirs = part_places(role, tile_cols, dest_plan, first_moving, held)
    other_core = lax.ppermute(same_core, "c", [(0, 1), (1, 0)])
    for_peer = pick_parts(theirs, same_core, other_core)
    from_peer = lax.ppermute(
        for_peer, GRP, [(first_moving, first_moving + 1), (first_moving + 1, first_moving)]
    )
    picked = pick_parts(mine, same_core, other_core) + from_peer
    picked = picked.reshape(adj_tiles.shape[0], slice_rows, feat_width)

    partial_value = lax.dot_general(
        picked, adj_tiles, (((0, 1), (0, 1)), ((), ())), preferred_element_type=jnp.float32
    ).astype(jnp.bfloat16)
    terms = exchange(partial_value, "x").reshape(lax.axis_size("x"), -1, block_rows)
    near = jnp.sum(terms.astype(jnp.float32), axis=0).astype(jnp.bfloat16)
    far = lax.ppermute(near, "zh", [(0, 1), (1, 0)])
    own_feats = (near.astype(jnp.float32) + far.astype(jnp.float32)).astype(jnp.bfloat16)
    aggregated = spread(own_feats, "x").reshape(feat_width, block_rows)

    projected = lax.dot_general(
        aggregated, weight, (((0,), (0,)), ((), ())), preferred_element_type=jnp.float32
    )
    sigmoid_part = jax.nn.sigmoid(projected)
    activated = (projected * sigmoid_part).astype(jnp.bfloat16)
    slope = sigmoid_part * (1.0 + projected * (1.0 - sigmoid_part))
    masked = (grad_out.astype(jnp.float32) * slope).astype(jnp.bfloat16)
    local_grad = jnp.dot(aggregated, masked, preferred_element_type=jnp.float32)

    ring_terms = exchange(local_grad, ("y", "c")).reshape(lax.axis_size(("y", "c")), -1, hid)
    line_terms = spread(jnp.sum(ring_terms, axis=0), "zl")
    own_grad = jnp.sum(line_terms.reshape((-1,) + ring_terms.shape[1:]), axis=0)
    weight_grad = spread(own_grad, ("y", "c")).reshape(feat_width, hid)
    return (activated, weight_grad)


def solution(mesh):
    fine_mesh = Mesh(mesh.devices.reshape(FINE), GRP + ROW)
    in_specs = (
        P(ROW, None),
        P(),
        P(None, GRP, ROW),
        P(ROW, None),
        P(ROW),
        P(ROW, None),
        P(),
    )
    out_specs = (P(ROW, None), P())
    return jax.shard_map(
        on_device, mesh=fine_mesh, in_specs=in_specs, out_specs=out_specs, check_vma=False
    )
```

```python
import functools

import jax
import jax.numpy as jnp
from jax import lax
from jax.experimental import pallas as pl
from jax.experimental.pallas import tpu as pltpu
from jax.sharding import Mesh, PartitionSpec as P

KEEP = 576
GRP = ("zh", "x")
ROW = ("y", "zl", "c")
FINE = (2, 4, 8, 6, 2)


def exchange(pieces, axes):
    return lax.all_to_all(pieces, axes, split_axis=0, concat_axis=0, tiled=True)


def spread(value, axes):
    copies = jnp.broadcast_to(value[None], (lax.axis_size(axes),) + value.shape)
    return exchange(copies, axes)


def added(terms):
    total = terms[0].astype(jnp.float32)
    for number in range(1, terms.shape[0]):
        total = total + terms[number].astype(jnp.float32)
    return total


def vmem():
    return pl.BlockSpec(memory_space=pltpu.VMEM)


def smem():
    return pl.BlockSpec(memory_space=pltpu.SMEM)


def contract_last(first, second):
    return lax.dot_general(
        first, second, (((1,), (1,)), ((), ())), preferred_element_type=jnp.float32
    )


def grid_of(shape, axis):
    return lax.broadcasted_iota(jnp.int32, shape, axis)


def places_kernel(
    first_moving, held, group_ref, core_ref, live_ref, slot_ref, plan_ref, column_ref, mine_ref, theirs_ref, sent_ref
):
    leaving, row_count = plan_ref.shape
    slot_count = column_ref.shape[1]
    half_rows = row_count // 2
    group, core, live = group_ref[0], core_ref[0], live_ref[0]
    half = jnp.maximum(group - first_moving, 0)

    plan = plan_ref[...]
    numbers = grid_of(plan.shape, 0) + 1
    for slot in range(slot_count):
        hits = jnp.where(plan == slot_ref[0, slot], numbers, 0)
        sent_ref[slot : slot + 1, :] = jnp.sum(hits.astype(jnp.float32), axis=0, keepdims=True)
    sent = sent_ref[...]

    square = (row_count, row_count)
    before = (grid_of(square, 1) < grid_of(square, 0)).astype(jnp.float32).astype(jnp.bfloat16)
    same = (grid_of(square, 1) == grid_of(square, 0)).astype(jnp.float32).astype(jnp.bfloat16)
    flags = jnp.where(sent > 0, 1.0, 0.0).astype(jnp.bfloat16)
    ranks = contract_last(before, flags).astype(jnp.int32)
    numbers = contract_last(same, sent.astype(jnp.bfloat16)).astype(jnp.int32) - 1

    source = grid_of(numbers.shape, 0)
    offset = (source >> 1) * held + jnp.where((source & 1) == core, 0, half_rows * held)
    local = numbers - half * held
    here = (numbers >= 0) & (local >= 0) & (local < held)
    none_held = row_count * held
    words = jnp.where(here, offset + local - none_held, 0)
    ranks = jnp.where(numbers >= 0, ranks, -1)

    columns = column_ref[...]
    column_base = (columns >> 1) * held + jnp.where((columns & 1) == core, 0, half_rows * held)
    dead = grid_of(columns.shape, 1) >= live
    for order in range(held):
        chosen = jnp.where(ranks == half * held + order, words, 0)
        moved = none_held + jnp.sum(chosen, axis=0, keepdims=True)
        stayed = column_base + order
        own = jnp.where(group >= first_moving, moved, stayed)
        mine_ref[order : order + 1, :] = jnp.where(dead, none_held, own)
        chosen = jnp.where(ranks == (1 - half) * held + order, words, 0)
        other = none_held + jnp.sum(chosen, axis=0, keepdims=True)
        theirs_ref[order : order + 1, :] = jnp.where(dead, none_held, other)


def part_places(role, columns, dest_plan, first_moving, held):
    shape = jax.ShapeDtypeStruct((held, columns.shape[1]), jnp.int32)
    return pl.pallas_call(
        functools.partial(places_kernel, first_moving, held),
        out_shape=(shape, shape),
        in_specs=[smem(), smem(), smem(), smem(), vmem(), vmem()],
        out_specs=(vmem(), vmem()),
        scratch_shapes=[pltpu.VMEM((columns.shape[1], dest_plan.shape[0]), jnp.float32)],
        cost_estimate=pl.CostEstimate(flops=4000000, bytes_accessed=50000, transcendentals=0),
    )(*role, columns, dest_plan.T, columns)


def pick_kernel(place_ref, first_ref, second_ref, out_ref, held_ref, sems):
    half = first_ref.shape[0]
    first = pltpu.make_async_copy(first_ref, held_ref.at[pl.ds(0, half)], sems.at[0])
    second = pltpu.make_async_copy(second_ref, held_ref.at[pl.ds(half, half)], sems.at[1])
    first.start()
    second.start()
    held_ref[2 * half] = jnp.zeros(held_ref.shape[1:], held_ref.dtype)
    first.wait()
    second.wait()
    orders, slots = place_ref.shape

    def one_slot(slot, carry):
        for order in range(orders):
            out_ref[slot * orders + order] = held_ref[place_ref[order, slot]]
        return carry

    lax.fori_loop(0, slots, one_slot, 0)


def pick_parts(places, first, second):
    part = first.shape[1:]
    count = places.shape[0] * places.shape[1]
    return pl.pallas_call(
        pick_kernel,
        out_shape=jax.ShapeDtypeStruct((count,) + part, first.dtype),
        in_specs=[smem()] + [pl.BlockSpec(memory_space=pl.ANY)] * 2,
        out_specs=vmem(),
        scratch_shapes=[
            pltpu.VMEM((2 * first.shape[0] + 8,) + part, first.dtype),
            pltpu.SemaphoreType.DMA((2,)),
        ],
        compiler_params=pltpu.CompilerParams(vmem_limit_bytes=8 * 1024 * 1024),
        cost_estimate=pl.CostEstimate(flops=1000000, bytes_accessed=3000000, transcendentals=0),
    )(places, first, second)


def on_device(features, dest_plan, adj_tiles, tile_cols, tile_count, grad_out, weight):
    block_rows, feat_width = features.shape
    hid = weight.shape[1]
    own_group = lax.axis_index(GRP)
    leaving = dest_plan.shape[1]
    part_rows = (block_rows - KEEP) // leaving
    slice_rows = block_rows // lax.axis_size(GRP)
    held = slice_rows // part_rows
    first_moving = KEEP // slice_rows
    part_shape = (-1, part_rows, feat_width)

    own_slice = lax.dynamic_slice_in_dim(features, own_group * slice_rows, slice_rows, 0)
    same_core = spread(spread(own_slice, "zl"), "y").reshape(part_shape)
    role = (own_group.reshape(1), lax.axis_index("c").reshape(1), tile_count)
    mine, theirs = part_places(role, tile_cols, dest_plan, first_moving, held)
    other_core = lax.ppermute(same_core, "c", [(0, 1), (1, 0)])
    for_peer = pick_parts(theirs, same_core, other_core)
    from_peer = lax.ppermute(
        for_peer, GRP, [(first_moving, first_moving + 1), (first_moving + 1, first_moving)]
    )
    picked = pick_parts(mine, same_core, other_core) + from_peer
    picked = picked.reshape(adj_tiles.shape[0], slice_rows, feat_width)

    partial_value = lax.dot_general(
        picked, adj_tiles, (((0, 1), (0, 1)), ((), ())), preferred_element_type=jnp.float32
    ).astype(jnp.bfloat16)
    terms = exchange(partial_value, "x").reshape(lax.axis_size("x"), -1, block_rows)
    near = added(terms).astype(jnp.bfloat16)
    far = lax.ppermute(near, "zh", [(0, 1), (1, 0)])
    own_feats = (near.astype(jnp.float32) + far.astype(jnp.float32)).astype(jnp.bfloat16)
    aggregated = spread(own_feats, "x").reshape(feat_width, block_rows)

    projected = lax.dot_general(
        aggregated, weight, (((0,), (0,)), ((), ())), preferred_element_type=jnp.float32
    )
    sigmoid_part = jax.nn.sigmoid(projected)
    activated = (projected * sigmoid_part).astype(jnp.bfloat16)
    slope = sigmoid_part * (1.0 + projected * (1.0 - sigmoid_part))
    masked = (grad_out.astype(jnp.float32) * slope).astype(jnp.bfloat16)
    local_grad = jnp.dot(aggregated, masked, preferred_element_type=jnp.float32)

    ring_terms = exchange(local_grad, ("y", "c")).reshape(lax.axis_size(("y", "c")), -1, hid)
    line_terms = spread(added(ring_terms), "zl")
    own_grad = added(line_terms.reshape((-1,) + ring_terms.shape[1:]))
    weight_grad = spread(own_grad, ("y", "c")).reshape(feat_width, hid)
    return (activated, weight_grad)


def solution(mesh):
    fine_mesh = Mesh(mesh.devices.reshape(FINE), GRP + ROW)
    in_specs = (
        P(ROW, None),
        P(),
        P(None, GRP, ROW),
        P(ROW, None),
        P(ROW),
        P(ROW, None),
        P(),
    )
    out_specs = (P(ROW, None), P())
    return jax.shard_map(
        on_device, mesh=fine_mesh, in_specs=in_specs, out_specs=out_specs, check_vma=False
    )
```

```python
import functools

import jax
import jax.numpy as jnp
from jax import lax
from jax.experimental import pallas as pl
from jax.experimental.pallas import tpu as pltpu
from jax.sharding import Mesh, PartitionSpec as P

KEEP = 576
GRP = ("zh", "x")
ROW = ("y", "zl", "c")
FINE = (2, 4, 8, 6, 2)


def exchange(pieces, axes):
    return lax.all_to_all(pieces, axes, split_axis=0, concat_axis=0, tiled=True)


def spread(value, axes):
    copies = jnp.broadcast_to(value[None], (lax.axis_size(axes),) + value.shape)
    return exchange(copies, axes)


def added(terms):
    total = terms[0].astype(jnp.float32)
    for number in range(1, terms.shape[0]):
        total = total + terms[number].astype(jnp.float32)
    return total


def vmem():
    return pl.BlockSpec(memory_space=pltpu.VMEM)


def smem():
    return pl.BlockSpec(memory_space=pltpu.SMEM)


def contract_last(first, second):
    return lax.dot_general(
        first, second, (((1,), (1,)), ((), ())), preferred_element_type=jnp.float32
    )


def grid_of(shape, axis):
    return lax.broadcasted_iota(jnp.int32, shape, axis)


def places_kernel(
    first_moving, held, group_ref, core_ref, live_ref, slot_ref, plan_ref, column_ref, mine_ref, theirs_ref, sent_ref
):
    leaving, row_count = plan_ref.shape
    slot_count = column_ref.shape[1]
    half_rows = row_count // 2
    group, core, live = group_ref[0], core_ref[0], live_ref[0]
    half = jnp.maximum(group - first_moving, 0)

    plan = plan_ref[...]
    numbers = grid_of(plan.shape, 0) + 1
    for slot in range(slot_count):
        hits = jnp.where(plan == slot_ref[0, slot], numbers, 0)
        sent_ref[slot : slot + 1, :] = jnp.sum(hits.astype(jnp.float32), axis=0, keepdims=True)
    sent = sent_ref[...]

    square = (row_count, row_count)
    before = (grid_of(square, 1) < grid_of(square, 0)).astype(jnp.float32).astype(jnp.bfloat16)
    same = (grid_of(square, 1) == grid_of(square, 0)).astype(jnp.float32).astype(jnp.bfloat16)
    flags = jnp.where(sent > 0, 1.0, 0.0).astype(jnp.bfloat16)
    ranks = contract_last(before, flags).astype(jnp.int32)
    numbers = contract_last(same, sent.astype(jnp.bfloat16)).astype(jnp.int32) - 1

    source = grid_of(numbers.shape, 0)
    offset = (source >> 1) * held + jnp.where((source & 1) == core, 0, half_rows * held)
    local = numbers - half * held
    here = (numbers >= 0) & (local >= 0) & (local < held)
    none_held = row_count * held
    words = jnp.where(here, offset + local - none_held, 0)
    ranks = jnp.where(numbers >= 0, ranks, -1)

    columns = column_ref[...]
    column_base = (columns >> 1) * held + jnp.where((columns & 1) == core, 0, half_rows * held)
    dead = grid_of(columns.shape, 1) >= live
    for order in range(held):
        chosen = jnp.where(ranks == half * held + order, words, 0)
        moved = none_held + jnp.sum(chosen, axis=0, keepdims=True)
        stayed = column_base + order
        own = jnp.where(group >= first_moving, moved, stayed)
        mine_ref[order : order + 1, :] = jnp.where(dead, none_held, own)
        chosen = jnp.where(ranks == (1 - half) * held + order, words, 0)
        other = none_held + jnp.sum(chosen, axis=0, keepdims=True)
        theirs_ref[order : order + 1, :] = jnp.where(dead, none_held, other)


def part_places(role, columns, dest_plan, first_moving, held):
    shape = jax.ShapeDtypeStruct((held, columns.shape[1]), jnp.int32)
    return pl.pallas_call(
        functools.partial(places_kernel, first_moving, held),
        out_shape=(shape, shape),
        in_specs=[smem(), smem(), smem(), smem(), vmem(), vmem()],
        out_specs=(vmem(), vmem()),
        scratch_shapes=[pltpu.VMEM((columns.shape[1], dest_plan.shape[0]), jnp.float32)],
        cost_estimate=pl.CostEstimate(flops=4000000, bytes_accessed=50000, transcendentals=0),
    )(*role, columns, dest_plan.T, columns)


def pick_kernel(place_ref, first_ref, second_ref, out_ref, held_ref, sems):
    half = first_ref.shape[0]
    first = pltpu.make_async_copy(first_ref, held_ref.at[pl.ds(0, half)], sems.at[0])
    second = pltpu.make_async_copy(second_ref, held_ref.at[pl.ds(half, half)], sems.at[1])
    first.start()
    second.start()
    held_ref[2 * half] = jnp.zeros(held_ref.shape[1:], held_ref.dtype)
    first.wait()
    second.wait()
    orders, slots = place_ref.shape

    def one_slot(slot, carry):
        for order in range(orders):
            out_ref[slot * orders + order] = held_ref[place_ref[order, slot]]
        return carry

    lax.fori_loop(0, slots, one_slot, 0)


def pick_parts(places, first, second):
    part = first.shape[1:]
    count = places.shape[0] * places.shape[1]
    return pl.pallas_call(
        pick_kernel,
        out_shape=jax.ShapeDtypeStruct((count,) + part, first.dtype),
        in_specs=[smem()] + [pl.BlockSpec(memory_space=pl.ANY)] * 2,
        out_specs=vmem(),
        scratch_shapes=[
            pltpu.VMEM((2 * first.shape[0] + 8,) + part, first.dtype),
            pltpu.SemaphoreType.DMA((2,)),
        ],
        compiler_params=pltpu.CompilerParams(vmem_limit_bytes=8 * 1024 * 1024),
        cost_estimate=pl.CostEstimate(flops=1000000, bytes_accessed=3000000, transcendentals=0),
    )(places, first, second)


def on_device(features, dest_plan, adj_tiles, tile_cols, tile_count, grad_out, weight):
    block_rows, feat_width = features.shape
    hid = weight.shape[1]
    own_group = lax.axis_index(GRP)
    leaving = dest_plan.shape[1]
    part_rows = (block_rows - KEEP) // leaving
    slice_rows = block_rows // lax.axis_size(GRP)
    held = slice_rows // part_rows
    first_moving = KEEP // slice_rows
    part_shape = (-1, part_rows, feat_width)

    own_slice = lax.dynamic_slice_in_dim(features, own_group * slice_rows, slice_rows, 0)
    same_core = spread(spread(own_slice, "zl"), "y").reshape(part_shape)
    role = (own_group.reshape(1), lax.axis_index("c").reshape(1), tile_count)
    mine, theirs = part_places(role, tile_cols, dest_plan, first_moving, held)
    other_core = lax.ppermute(same_core, "c", [(0, 1), (1, 0)])
    for_peer = pick_parts(theirs, same_core, other_core)
    from_peer = lax.ppermute(
        for_peer, GRP, [(first_moving, first_moving + 1), (first_moving + 1, first_moving)]
    )
    picked = pick_parts(mine, same_core, other_core) + from_peer
    picked = picked.reshape(adj_tiles.shape[0], slice_rows, feat_width)

    partial_value = lax.dot_general(
        picked, adj_tiles, (((0, 1), (0, 1)), ((), ())), preferred_element_type=jnp.float32
    ).astype(jnp.bfloat16)
    terms = exchange(partial_value, "x").reshape(lax.axis_size("x"), -1, block_rows)
    near = added(terms).astype(jnp.bfloat16)
    far = lax.ppermute(near, "zh", [(0, 1), (1, 0)])
    own_feats = (near.astype(jnp.float32) + far.astype(jnp.float32)).astype(jnp.bfloat16)
    aggregated = spread(own_feats, "x").reshape(feat_width, block_rows)

    projected = lax.dot_general(
        aggregated, weight, (((0,), (0,)), ((), ())), preferred_element_type=jnp.float32
    )
    sigmoid_part = jax.nn.sigmoid(projected)
    activated = (projected * sigmoid_part).astype(jnp.bfloat16)
    slope = sigmoid_part * (1.0 + projected * (1.0 - sigmoid_part))
    masked = (grad_out.astype(jnp.float32) * slope).astype(jnp.bfloat16)
    local_grad = jnp.dot(aggregated, masked, preferred_element_type=jnp.float32)

    ring_terms = exchange(local_grad.astype(jnp.bfloat16), ("y", "c")).reshape(lax.axis_size(("y", "c")), -1, hid)
    line_terms = spread(added(ring_terms), "zl")
    own_grad = added(line_terms.reshape((-1,) + ring_terms.shape[1:]))
    weight_grad = spread(own_grad, ("y", "c")).reshape(feat_width, hid)
    return (activated, weight_grad)


def solution(mesh):
    fine_mesh = Mesh(mesh.devices.reshape(FINE), GRP + ROW)
    in_specs = (
        P(ROW, None),
        P(),
        P(None, GRP, ROW),
        P(ROW, None),
        P(ROW),
        P(ROW, None),
        P(),
    )
    out_specs = (P(ROW, None), P())
    return jax.shard_map(
        on_device, mesh=fine_mesh, in_specs=in_specs, out_specs=out_specs, check_vma=False
    )
```

```python
import functools

import jax
import jax.numpy as jnp
from jax import lax
from jax.experimental import pallas as pl
from jax.experimental.pallas import tpu as pltpu
from jax.sharding import Mesh, PartitionSpec as P

KEEP = 576
GRP = ("zh", "x")
ROW = ("y", "zl", "c")
FINE = (2, 4, 8, 6, 2)


def exchange(pieces, axes):
    return lax.all_to_all(pieces, axes, split_axis=0, concat_axis=0, tiled=True)


def spread(value, axes):
    copies = jnp.broadcast_to(value[None], (lax.axis_size(axes),) + value.shape)
    return exchange(copies, axes)


def added(terms):
    total = terms[0].astype(jnp.float32)
    for number in range(1, terms.shape[0]):
        total = total + terms[number].astype(jnp.float32)
    return total


def vmem():
    return pl.BlockSpec(memory_space=pltpu.VMEM)


def smem():
    return pl.BlockSpec(memory_space=pltpu.SMEM)


def contract_last(first, second):
    return lax.dot_general(
        first, second, (((1,), (1,)), ((), ())), preferred_element_type=jnp.float32
    )


def grid_of(shape, axis):
    return lax.broadcasted_iota(jnp.int32, shape, axis)


def places_kernel(
    first_moving, held, group_ref, core_ref, live_ref, slot_ref, plan_ref, column_ref, mine_ref, theirs_ref, sent_ref
):
    leaving, row_count = plan_ref.shape
    slot_count = column_ref.shape[1]
    half_rows = row_count // 2
    group, core, live = group_ref[0], core_ref[0], live_ref[0]
    half = jnp.maximum(group - first_moving, 0)

    plan = plan_ref[...]
    numbers = grid_of(plan.shape, 0) + 1
    for slot in range(slot_count):
        hits = jnp.where(plan == slot_ref[0, slot], numbers, 0)
        sent_ref[slot : slot + 1, :] = jnp.sum(hits.astype(jnp.float32), axis=0, keepdims=True)
    sent = sent_ref[...]

    square = (row_count, row_count)
    before = (grid_of(square, 1) < grid_of(square, 0)).astype(jnp.float32).astype(jnp.bfloat16)
    same = (grid_of(square, 1) == grid_of(square, 0)).astype(jnp.float32).astype(jnp.bfloat16)
    flags = jnp.where(sent > 0, 1.0, 0.0).astype(jnp.bfloat16)
    ranks = contract_last(before, flags).astype(jnp.int32)
    numbers = contract_last(same, sent.astype(jnp.bfloat16)).astype(jnp.int32) - 1

    source = grid_of(numbers.shape, 0)
    offset = (source >> 1) * held + jnp.where((source & 1) == core, 0, half_rows * held)
    local = numbers - half * held
    here = (numbers >= 0) & (local >= 0) & (local < held)
    none_held = row_count * held
    words = jnp.where(here, offset + local - none_held, 0)
    ranks = jnp.where(numbers >= 0, ranks, -1)

    columns = column_ref[...]
    column_base = (columns >> 1) * held + jnp.where((columns & 1) == core, 0, half_rows * held)
    dead = grid_of(columns.shape, 1) >= live
    for order in range(held):
        chosen = jnp.where(ranks == half * held + order, words, 0)
        moved = none_held + jnp.sum(chosen, axis=0, keepdims=True)
        stayed = column_base + order
        own = jnp.where(group >= first_moving, moved, stayed)
        mine_ref[order : order + 1, :] = jnp.where(dead, none_held, own)
        chosen = jnp.where(ranks == (1 - half) * held + order, words, 0)
        other = none_held + jnp.sum(chosen, axis=0, keepdims=True)
        theirs_ref[order : order + 1, :] = jnp.where(dead, none_held, other)


def part_places(role, columns, dest_plan, first_moving, held):
    shape = jax.ShapeDtypeStruct((held, columns.shape[1]), jnp.int32)
    return pl.pallas_call(
        functools.partial(places_kernel, first_moving, held),
        out_shape=(shape, shape),
        in_specs=[smem(), smem(), smem(), smem(), vmem(), vmem()],
        out_specs=(vmem(), vmem()),
        scratch_shapes=[pltpu.VMEM((columns.shape[1], dest_plan.shape[0]), jnp.float32)],
        cost_estimate=pl.CostEstimate(flops=4000000, bytes_accessed=50000, transcendentals=0),
    )(*role, columns, dest_plan.T, columns)


def pick_kernel(list_ref, first_ref, second_ref, out_ref, held_ref, place_ref, sems):
    half = first_ref.shape[0]
    first = pltpu.make_async_copy(first_ref, held_ref.at[pl.ds(0, half)], sems.at[0])
    second = pltpu.make_async_copy(second_ref, held_ref.at[pl.ds(half, half)], sems.at[1])
    listed = pltpu.make_async_copy(list_ref, place_ref, sems.at[2])
    listed.start()
    first.start()
    second.start()
    held_ref[2 * half] = jnp.zeros(held_ref.shape[1:], held_ref.dtype)
    listed.wait()
    first.wait()
    second.wait()
    orders, slots = place_ref.shape

    def one_slot(slot, carry):
        for order in range(orders):
            out_ref[slot * orders + order] = held_ref[place_ref[order, slot]]
        return carry

    lax.fori_loop(0, slots, one_slot, 0)


def pick_parts(places, first, second):
    part = first.shape[1:]
    count = places.shape[0] * places.shape[1]
    return pl.pallas_call(
        pick_kernel,
        out_shape=jax.ShapeDtypeStruct((count,) + part, first.dtype),
        in_specs=[pl.BlockSpec(memory_space=pl.ANY)] * 3,
        out_specs=vmem(),
        scratch_shapes=[
            pltpu.VMEM((2 * first.shape[0] + 8,) + part, first.dtype),
            pltpu.SMEM(places.shape, jnp.int32),
            pltpu.SemaphoreType.DMA((3,)),
        ],
        compiler_params=pltpu.CompilerParams(vmem_limit_bytes=8 * 1024 * 1024),
        cost_estimate=pl.CostEstimate(flops=1000000, bytes_accessed=3000000, transcendentals=0),
    )(places, first, second)


def on_device(features, dest_plan, adj_tiles, tile_cols, tile_count, grad_out, weight):
    block_rows, feat_width = features.shape
    hid = weight.shape[1]
    own_group = lax.axis_index(GRP)
    leaving = dest_plan.shape[1]
    part_rows = (block_rows - KEEP) // leaving
    slice_rows = block_rows // lax.axis_size(GRP)
    held = slice_rows // part_rows
    first_moving = KEEP // slice_rows
    part_shape = (-1, part_rows, feat_width)

    own_slice = lax.dynamic_slice_in_dim(features, own_group * slice_rows, slice_rows, 0)
    same_core = spread(spread(own_slice, "zl"), "y").reshape(part_shape)
    role = (own_group.reshape(1), lax.axis_index("c").reshape(1), tile_count)
    mine, theirs = part_places(role, tile_cols, dest_plan, first_moving, held)
    other_core = lax.ppermute(same_core, "c", [(0, 1), (1, 0)])
    for_peer = pick_parts(theirs, same_core, other_core)
    from_peer = lax.ppermute(
        for_peer, GRP, [(first_moving, first_moving + 1), (first_moving + 1, first_moving)]
    )
    picked = pick_parts(mine, same_core, other_core) + from_peer
    picked = picked.reshape(adj_tiles.shape[0], slice_rows, feat_width)

    partial_value = lax.dot_general(
        picked, adj_tiles, (((0, 1), (0, 1)), ((), ())), preferred_element_type=jnp.float32
    ).astype(jnp.bfloat16)
    terms = exchange(partial_value, "x").reshape(lax.axis_size("x"), -1, block_rows)
    near = added(terms).astype(jnp.bfloat16)
    far = lax.ppermute(near, "zh", [(0, 1), (1, 0)])
    own_feats = (near.astype(jnp.float32) + far.astype(jnp.float32)).astype(jnp.bfloat16)
    aggregated = spread(own_feats, "x").reshape(feat_width, block_rows)

    projected = lax.dot_general(
        aggregated, weight, (((0,), (0,)), ((), ())), preferred_element_type=jnp.float32
    )
    sigmoid_part = jax.nn.sigmoid(projected)
    activated = (projected * sigmoid_part).astype(jnp.bfloat16)
    slope = sigmoid_part * (1.0 + projected * (1.0 - sigmoid_part))
    masked = (grad_out.astype(jnp.float32) * slope).astype(jnp.bfloat16)
    local_grad = jnp.dot(aggregated, masked, preferred_element_type=jnp.float32)

    ring_terms = exchange(local_grad.astype(jnp.bfloat16), ("y", "c")).reshape(lax.axis_size(("y", "c")), -1, hid)
    line_terms = spread(added(ring_terms), "zl")
    own_grad = added(line_terms.reshape((-1,) + ring_terms.shape[1:]))
    weight_grad = spread(own_grad, ("y", "c")).reshape(feat_width, hid)
    return (activated, weight_grad)


def solution(mesh):
    fine_mesh = Mesh(mesh.devices.reshape(FINE), GRP + ROW)
    in_specs = (
        P(ROW, None),
        P(),
        P(None, GRP, ROW),
        P(ROW, None),
        P(ROW),
        P(ROW, None),
        P(),
    )
    out_specs = (P(ROW, None), P())
    return jax.shard_map(
        on_device, mesh=fine_mesh, in_specs=in_specs, out_specs=out_specs, check_vma=False
    )
```

```python
import functools

import jax
import jax.numpy as jnp
from jax import lax
from jax.experimental import pallas as pl
from jax.experimental.pallas import tpu as pltpu
from jax.sharding import Mesh, PartitionSpec as P

KEEP = 576
GRP = ("zh", "x")
ROW = ("y", "zl", "c")
FINE = (2, 4, 8, 6, 2)


def exchange(pieces, axes):
    return lax.all_to_all(pieces, axes, split_axis=0, concat_axis=0, tiled=True)


def spread(value, axes):
    copies = jnp.broadcast_to(value[None], (lax.axis_size(axes),) + value.shape)
    return exchange(copies, axes)


def added(terms):
    total = terms[0].astype(jnp.float32)
    for number in range(1, terms.shape[0]):
        total = total + terms[number].astype(jnp.float32)
    return total


def vmem():
    return pl.BlockSpec(memory_space=pltpu.VMEM)


def smem():
    return pl.BlockSpec(memory_space=pltpu.SMEM)


def contract_last(first, second):
    return lax.dot_general(
        first, second, (((1,), (1,)), ((), ())), preferred_element_type=jnp.float32
    )


def grid_of(shape, axis):
    return lax.broadcasted_iota(jnp.int32, shape, axis)


def places_kernel(
    first_moving, held, group_ref, core_ref, live_ref, slot_ref, plan_ref, column_ref, mine_ref, theirs_ref, sent_ref
):
    leaving, row_count = plan_ref.shape
    slot_count = column_ref.shape[1]
    half_rows = row_count // 2
    group, core, live = group_ref[0], core_ref[0], live_ref[0]
    half = jnp.maximum(group - first_moving, 0)

    plan = plan_ref[...]
    numbers = grid_of(plan.shape, 0) + 1
    for slot in range(slot_count):
        hits = jnp.where(plan == slot_ref[0, slot], numbers, 0)
        sent_ref[slot : slot + 1, :] = jnp.sum(hits.astype(jnp.float32), axis=0, keepdims=True)
    sent = sent_ref[...]

    square = (row_count, row_count)
    before = (grid_of(square, 1) < grid_of(square, 0)).astype(jnp.float32).astype(jnp.bfloat16)
    same = (grid_of(square, 1) == grid_of(square, 0)).astype(jnp.float32).astype(jnp.bfloat16)
    flags = jnp.where(sent > 0, 1.0, 0.0).astype(jnp.bfloat16)
    ranks = contract_last(before, flags).astype(jnp.int32)
    numbers = contract_last(same, sent.astype(jnp.bfloat16)).astype(jnp.int32) - 1

    source = grid_of(numbers.shape, 0)
    offset = (source >> 1) * held + jnp.where((source & 1) == core, 0, half_rows * held)
    local = numbers - half * held
    here = (numbers >= 0) & (local >= 0) & (local < held)
    none_held = row_count * held
    words = jnp.where(here, offset + local - none_held, 0)
    ranks = jnp.where(numbers >= 0, ranks, -1)

    columns = column_ref[...]
    column_base = (columns >> 1) * held + jnp.where((columns & 1) == core, 0, half_rows * held)
    dead = grid_of(columns.shape, 1) >= live
    for order in range(held):
        chosen = jnp.where(ranks == half * held + order, words, 0)
        moved = none_held + jnp.sum(chosen, axis=0, keepdims=True)
        stayed = column_base + order
        own = jnp.where(group >= first_moving, moved, stayed)
        mine_ref[order : order + 1, :] = jnp.where(dead, none_held, own)
        chosen = jnp.where(ranks == (1 - half) * held + order, words, 0)
        other = none_held + jnp.sum(chosen, axis=0, keepdims=True)
        theirs_ref[order : order + 1, :] = jnp.where(dead, none_held, other)


def part_places(role, columns, dest_plan, first_moving, held):
    shape = jax.ShapeDtypeStruct((held, columns.shape[1]), jnp.int32)
    return pl.pallas_call(
        functools.partial(places_kernel, first_moving, held),
        out_shape=(shape, shape),
        in_specs=[smem(), smem(), smem(), smem(), vmem(), vmem()],
        out_specs=(vmem(), vmem()),
        scratch_shapes=[pltpu.VMEM((columns.shape[1], dest_plan.shape[0]), jnp.float32)],
        cost_estimate=pl.CostEstimate(flops=4000000, bytes_accessed=50000, transcendentals=0),
    )(*role, columns, dest_plan.T, columns)


def pick_kernel(list_ref, first_ref, second_ref, out_ref, held_ref, place_ref, sems):
    half = first_ref.shape[0]
    first = pltpu.make_async_copy(first_ref, held_ref.at[pl.ds(0, half)], sems.at[0])
    second = pltpu.make_async_copy(second_ref, held_ref.at[pl.ds(half, half)], sems.at[1])
    listed = pltpu.make_async_copy(list_ref, place_ref, sems.at[2])
    listed.start()
    first.start()
    second.start()
    held_ref[2 * half] = jnp.zeros(held_ref.shape[1:], held_ref.dtype)
    listed.wait()
    first.wait()
    second.wait()
    orders, slots = place_ref.shape

    def one_slot(slot, carry):
        for order in range(orders):
            out_ref[slot * orders + order] = held_ref[place_ref[order, slot]]
        return carry

    lax.fori_loop(0, slots, one_slot, 0)


def pick_parts(places, first, second):
    part = first.shape[1:]
    count = places.shape[0] * places.shape[1]
    return pl.pallas_call(
        pick_kernel,
        out_shape=jax.ShapeDtypeStruct((count,) + part, first.dtype),
        in_specs=[pl.BlockSpec(memory_space=pl.ANY)] * 3,
        out_specs=vmem(),
        scratch_shapes=[
            pltpu.VMEM((2 * first.shape[0] + 8,) + part, first.dtype),
            pltpu.SMEM(places.shape, jnp.int32),
            pltpu.SemaphoreType.DMA((3,)),
        ],
        compiler_params=pltpu.CompilerParams(vmem_limit_bytes=8 * 1024 * 1024),
        cost_estimate=pl.CostEstimate(flops=1000000, bytes_accessed=3000000, transcendentals=0),
    )(places, first, second)


def on_device(features, dest_plan, adj_tiles, tile_cols, tile_count, grad_out, weight):
    block_rows, feat_width = features.shape
    hid = weight.shape[1]
    own_group = lax.axis_index(GRP)
    leaving = dest_plan.shape[1]
    part_rows = (block_rows - KEEP) // leaving
    slice_rows = block_rows // lax.axis_size(GRP)
    held = slice_rows // part_rows
    first_moving = KEEP // slice_rows
    part_shape = (-1, part_rows, feat_width)

    own_slice = lax.dynamic_slice_in_dim(features, own_group * slice_rows, slice_rows, 0)
    same_core = spread(spread(own_slice, "zl"), "y").reshape(part_shape)
    role = (own_group.reshape(1), lax.axis_index("c").reshape(1), tile_count)
    mine, theirs = part_places(role, tile_cols, dest_plan, first_moving, held)
    other_core = lax.ppermute(same_core, "c", [(0, 1), (1, 0)])
    for_peer = pick_parts(theirs, same_core, other_core)
    from_peer = lax.ppermute(
        for_peer, GRP, [(first_moving, first_moving + 1), (first_moving + 1, first_moving)]
    )
    picked = pick_parts(mine, same_core, other_core) + from_peer
    picked = picked.reshape(adj_tiles.shape[0], slice_rows, feat_width)

    partial_value = lax.dot_general(
        picked, adj_tiles, (((0, 1), (0, 1)), ((), ())), preferred_element_type=jnp.float32
    ).astype(jnp.bfloat16)
    terms = exchange(partial_value, "x").reshape(lax.axis_size("x"), -1, block_rows)
    near = added(terms).astype(jnp.bfloat16)
    far = lax.ppermute(near, "zh", [(0, 1), (1, 0)])
    own_feats = (near.astype(jnp.float32) + far.astype(jnp.float32)).astype(jnp.bfloat16)
    aggregated = spread(own_feats, "x").reshape(feat_width, block_rows)

    projected = lax.dot_general(
        aggregated, weight, (((0,), (0,)), ((), ())), preferred_element_type=jnp.float32
    )
    sigmoid_part = jax.nn.sigmoid(projected)
    activated = (projected * sigmoid_part).astype(jnp.bfloat16)
    slope = sigmoid_part * (1.0 + projected * (1.0 - sigmoid_part))
    masked = (grad_out.astype(jnp.float32) * slope).astype(jnp.bfloat16)
    local_grad = jnp.dot(aggregated, masked, preferred_element_type=jnp.float32)

    ring_terms = exchange(local_grad.astype(jnp.bfloat16), ("y", "c")).reshape(lax.axis_size(("y", "c")), -1, hid)
    line_terms = spread(added(ring_terms).astype(jnp.bfloat16), "zl")
    own_grad = added(line_terms.reshape((-1,) + ring_terms.shape[1:]))
    weight_grad = spread(own_grad, ("y", "c")).reshape(feat_width, hid)
    return (activated, weight_grad)


def solution(mesh):
    fine_mesh = Mesh(mesh.devices.reshape(FINE), GRP + ROW)
    in_specs = (
        P(ROW, None),
        P(),
        P(None, GRP, ROW),
        P(ROW, None),
        P(ROW),
        P(ROW, None),
        P(),
    )
    out_specs = (P(ROW, None), P())
    return jax.shard_map(
        on_device, mesh=fine_mesh, in_specs=in_specs, out_specs=out_specs, check_vma=False
    )
```
